32 devices in a mesh: groups: 2 (over x), blk: 16 (over z, y, core).
Axes of the slice: x: 2, y: 2, z: 4, core: 2. Of those that a mesh axis runs over, the one named last changes fastest.
Arguments:
- a_blocks: bfloat16 [128, 5, 3, 128, 128], P(('groups', 'blk')), parts along dimension 0, may hold values from -6 to 6
- a_cols: int32 [128, 5, 3], P(('groups', 'blk')), parts along dimension 0, may hold values from 0 to 63, as said below
- b_blocks: bfloat16 [128, 15, 128, 128], P(('groups', 'blk')), parts along dimension 0, may hold values from -0.5 to 0.5
- b_cols: int32 [128, 15], P(('groups', 'blk')), parts along dimension 0, may hold values from 0 to 63, as said below
- c_cols: int32 [128, 15], P(('groups', 'blk')), parts along dimension 0, may hold values from 0 to 63, as said below
Outputs:
- c_blocks: bfloat16 [128, 15, 128, 128], P(('groups', 'blk')), parts along dimension 0
The draws below stay inside these ranges and needn't reach their ends.
There are 2 independent parts, one for each index of `groups`. The reference program is written for one: setup_inputs(seed, part) draws one part's arguments, and reference() takes and returns one part's arrays. A program takes and returns all parts, laid end to end along the dimension named above; each array names one. Nothing has to cross between parts.
Inputs may be any that keep to these rules, and one draw needn't show every extreme that they name: Block row i belongs to device i // 4; a_cols[i, h, s] is a block column of device (i // 4 + h - 2) mod (16), that is one of its 4 consecutive block columns, and the 3 entries of a_cols[i, h] differ. `b_cols`: the 15 entries of a row k differ and lie among the 20 block columns of the devices k // 4 - 2 to k // 4 + 2, cyclically. `c_cols`: the 15 entries of a row i differ and lie among the 20 block columns of the devices i // 4 - 2 to i // 4 + 2, cyclically.
All inputs are finite; a program needn't handle non-finite values.
Results may differ from the reference program's by a relative error of at most 0.001.
Values may be sent and summed in bfloat16 or wider, within the bound.
No kernel may reach another device: no remote copies, remote signals or barrier semaphores. Data moves between devices by JAX's collectives and lax.ppermute only.
A program may use at most 128 MiB of HBM per device.

```python
import jax
import jax.numpy as jnp
from jax import lax

BS = 128
RB = 4
HOPS = 2
SL = 3
BNZ = 15
CNZ = 15
NB = 64


def distinct_positions(key, rows, picked, span):
    scores = jax.random.randint(key, (rows, span), 0, 1048576) * span + jnp.arange(span, dtype=jnp.int32)[None, :]
    order = jnp.argsort(scores, axis=1)
    return order[:, :picked].astype(jnp.int32)


def window_cols(key, picked):
    span = (2 * HOPS + 1) * RB
    positions = distinct_positions(key, NB, picked, span)
    owner_id = jnp.arange(NB, dtype=jnp.int32) // RB
    return jnp.remainder((owner_id[:, None] - HOPS) * RB + positions, NB).astype(jnp.int32)


def draw_a_cols(key, part):
    key = jax.random.fold_in(key, 11)
    hops_all = 2 * HOPS + 1
    positions = distinct_positions(key, NB * hops_all, SL, RB).reshape(NB, hops_all, SL)
    owner_id = jnp.arange(NB, dtype=jnp.int32) // RB
    shifts = jnp.arange(hops_all, dtype=jnp.int32) - HOPS
    target = jnp.remainder(owner_id[:, None] + shifts[None, :], NB // RB)
    return (target[:, :, None] * RB + positions).astype(jnp.int32)


def draw_b_cols(key, part):
    key = jax.random.fold_in(key, 23)
    return window_cols(key, BNZ)


def draw_c_cols(key, part):
    key = jax.random.fold_in(key, 37)
    return window_cols(key, CNZ)


def block_scale(own_key, extent, shards, low, high):
    def one(dim, parts):
        draws = jax.random.uniform(jax.random.fold_in(jax.random.fold_in(own_key, 6), dim), (parts,), jnp.float32, low / len(shards), high / len(shards))
        return jnp.repeat(jnp.exp(draws), extent[dim] // parts).reshape((-1,) + (1,) * (len(extent) - dim - 1))

    loudness = one(*shards[0])
    for cut in shards[1:]:
        loudness = loudness * one(*cut)
    return loudness


def scatter_about(key, dims, deviation, most, pieces=(), kind=jnp.bfloat16):
    array = jax.random.normal(key, dims, jnp.float32) * deviation
    if len(pieces) > 0:
        array = block_scale(key, dims, pieces, -0.22, 0.18) * array
    return jnp.clip(array, min=-most, max=most).astype(kind)


def setup_inputs(seed: int = 0, part: int = 0) -> dict:
    splits = jax.random.split(jax.random.key(seed), 6)
    part_splits = jax.random.split(jax.random.fold_in(splits[5], part), 6)
    a_blocks = scatter_about(part_splits[0], (NB, 2 * HOPS + 1, SL, BS, BS), 0.4, 6.0, ((0, 16),))
    a_cols = draw_a_cols(jax.random.fold_in(jax.random.fold_in(splits[5], part), 71), part)
    b_blocks = scatter_about(part_splits[2], (NB, BNZ, BS, BS), BS ** -0.5, 0.5, ((0, 16),))
    b_cols = draw_b_cols(jax.random.fold_in(jax.random.fold_in(splits[5], part), 71), part)
    c_cols = draw_c_cols(jax.random.fold_in(jax.random.fold_in(splits[5], part), 71), part)
    return dict(a_blocks=a_blocks, a_cols=a_cols, b_blocks=b_blocks, b_cols=b_cols, c_cols=c_cols)


def contribute(a_piece, a_list, c_rows, b_rows, b_rows_cols):
    row_count = b_rows.shape[0]
    slot_width = b_rows.shape[1]
    block_size = b_rows.shape[2]
    position = a_list % row_count
    onehot = (position[:, :, None] == jnp.arange(row_count, dtype=jnp.int32)[None, None, :]).astype(jnp.int32)
    cols_seen = jnp.sum(onehot[:, :, :, None] * b_rows_cols[None, None, :, :], axis=2)
    matches = cols_seen[:, :, None, :] == c_rows[:, None, :, None]
    flat_index = position[:, :, None, None] * slot_width + jnp.arange(slot_width, dtype=jnp.int32)[None, None, None, :]
    pointer = jnp.sum(jnp.where(matches, flat_index, 0), axis=3) + jnp.where(jnp.any(matches, axis=3), 0, row_count * slot_width)
    bank_rows = jnp.concatenate([b_rows.reshape(row_count * slot_width, block_size, block_size), jnp.zeros((1, block_size, block_size), b_rows.dtype)], axis=0)
    chosen = jnp.take(bank_rows, pointer.astype(jnp.int32), axis=0)
    return jnp.einsum("isxy,ismyz->imxz", a_piece.astype(jnp.float32), chosen.astype(jnp.float32))


def reference(a_blocks, a_cols, b_blocks, b_cols, c_cols):
    devices = NB // RB

    def owner_rows(owner_id):
        first_row = (owner_id * RB).astype(jnp.int32)
        a_rows = lax.dynamic_slice_in_dim(a_blocks, first_row, RB, 0)
        a_lists = lax.dynamic_slice_in_dim(a_cols, first_row, RB, 0)
        c_rows = lax.dynamic_slice_in_dim(c_cols, first_row, RB, 0)
        summed = jnp.zeros((RB, CNZ, BS, BS), jnp.float32)
        for h in range(2 * HOPS + 1):
            source = (jnp.remainder(owner_id + h - HOPS, devices) * RB).astype(jnp.int32)
            b_rows = lax.dynamic_slice_in_dim(b_blocks, source, RB, 0)
            b_rows_cols = lax.dynamic_slice_in_dim(b_cols, source, RB, 0)
            summed = summed + contribute(a_rows[:, h], a_lists[:, h], c_rows, b_rows, b_rows_cols)
        return summed.astype(jnp.bfloat16)

    result = lax.map(owner_rows, jnp.arange(devices, dtype=jnp.int32))
    return result.reshape(NB, CNZ, BS, BS)
```

```python
import functools

import jax
import jax.numpy as jnp
from jax import lax
from jax.experimental import pallas as pl
from jax.experimental.pallas import tpu as pltpu
from jax.sharding import PartitionSpec as P

HOPS = 2
NOTE = 16
SHARES = (10, 10, 10, 10, 10, 10)
COST = 2_000_000


def permuted(block, route):
    count = lax.axis_size("blk")
    return lax.ppermute(block, "blk", [(i, route(i) % count) for i in range(count)])


def other_core(i):
    return i ^ 1


def across_y(i):
    return i ^ 2


def across_z(i):
    return i - 4 if i & 2 else i + 4


def chunk_bounds(total):
    edges = [0]
    for share in SHARES:
        edges.append(edges[-1] + share)
    return [e * total // edges[-1] for e in edges]


def pack_kernel(d_count, rb, cols, blocks, out, out_sem):
    bs = blocks.shape[-1]
    slots = cols.shape[1]
    rows = out.shape[0] - NOTE
    copy = pltpu.make_async_copy(blocks.at[pl.ds(0, rows)], out.at[pl.ds(0, rows)], out_sem)
    copy.start()
    corner = (lax.axis_index("blk") - HOPS + d_count) % d_count * rb
    at = cols[...] - corner
    at = jnp.where(at < 0, at + d_count * rb, at).astype(jnp.float32)
    at = jnp.concatenate([at, jnp.zeros((rb, bs - slots), jnp.float32)], axis=1)
    at = jnp.concatenate([at, jnp.zeros((NOTE - rb, bs), jnp.float32)], axis=0)
    out[rows : rows + NOTE, :] = at.astype(out.dtype)
    copy.wait()


def add_kernel(pieces, names, first, last, noted, d_count, rb, *refs):
    at = dict(zip(names, refs))
    a_dense, total = at["a_dense"], at["total"]
    bs = a_dense.shape[2] // rb
    span = (2 * HOPS + 1) * rb

    me = lax.axis_index("blk")
    core, y = me % 2, (me // 2) % 2
    corner = (me - HOPS + d_count) % d_count * rb

    def place(col):
        return (col - corner + d_count * rb) % (d_count * rb)

    def lanes(block):
        return pl.ds(pl.multiple_of(block * bs, bs), bs)

    hop_of = {
        "own": 0,
        "near": 1 - 2 * core,
        "far_y": 2 - 4 * y,
        "far_z": 4 * y - 2,
        "side": 2 * core - 1,
    }
    side_is_y = (y + core) % 2 == 1

    if first:
        a_blocks, a_cols, a_sem = at["a_blocks"], at["a_cols"], at["a_sem"]
        copies = [pltpu.make_async_copy(at["b_hbm"], at["own"], at["b_sem"])]
        copies[0].start()
        hops_all, sl = a_blocks.shape[1], a_blocks.shape[2]
        for h in range(hops_all):
            for i in range(rb):
                rows = pl.ds(i * bs, bs)
                gap = rb * (rb - 1) // 2
                for s in range(sl):
                    to = a_cols[s, i, h] % rb
                    gap -= to
                    copies.append(
                        pltpu.make_async_copy(
                            a_blocks.at[i, h, s], a_dense.at[h, rows, lanes(to)], a_sem
                        )
                    )
                    copies[-1].start()
                a_dense[h, rows, lanes(gap)] = jnp.zeros((bs, bs), a_dense.dtype)
        total[...] = jnp.zeros_like(total)
        for c in copies:
            c.wait()

    fetches = []
    for kind in noted:
        notes = [
            at[name][at[name].shape[0] - NOTE :, :].astype(jnp.float32).astype(jnp.int32)
            for name in noted[kind]
        ]
        found = notes[0] if len(notes) == 1 else jnp.where(side_is_y, *notes)
        found = found + hop_of[kind] * rb
        found = jnp.where((found >= 0) & (found < span), found, span)
        at[f"out_{kind}"][...] = found
        fetches.append(pltpu.make_async_copy(at[f"out_{kind}"], at[f"note_{kind}"], at["n_sem"]))
        fetches[-1].start()
    for fetch in fetches:
        fetch.wait()

    for kind, begin, count, source, other in pieces:
        hop = hop_of[kind] + HOPS
        local = kind == "own"
        slots = at["cols_own" if local else "notes_like"].shape[1]
        for n in range(count):
            row, slot = divmod(begin + n, slots)
            if local:
                to = jnp.minimum(place(at["cols_own"][row, slot]), span)
                block = at[source][n]
            else:
                to = at[f"note_{kind}"][row, slot]
                part = slice(n * bs, (n + 1) * bs)
                block = at[source][part, :]
                if other is not None:
                    block = jnp.where(side_is_y, block, at[other][part, :])
            total[:, lanes(to)] += jnp.dot(
                a_dense[hop, :, row * bs : (row + 1) * bs],
                block,
                preferred_element_type=jnp.float32,
            )

    if last:
        c_cols, staged = at["c_cols"], at["staged"]
        sends = []
        for i in range(rb):
            for m in range(c_cols.shape[1]):
                block = total[i * bs : (i + 1) * bs, lanes(place(c_cols[i, m]))]
                staged[i, m] = block.astype(staged.dtype)
            sends.append(pltpu.make_async_copy(staged.at[i], at["out"].at[i], at["o_sem"].at[i]))
            sends[-1].start()
        for c in sends:
            c.wait()


def per_device(a_blocks, a_cols, b_blocks, b_cols, c_cols):
    rb, hops_all, sl, bs, _ = a_blocks.shape
    m_count, slots = c_cols.shape[1], b_cols.shape[1]
    span = hops_all * rb
    d_count = lax.axis_size("blk")
    flat_b = b_blocks.reshape(rb * slots, bs, bs)
    after = lax.optimization_barrier
    in_hbm = functools.partial(pltpu.with_memory_space_constraint, memory_space=pltpu.HBM)

    any_space = pl.BlockSpec(memory_space=pl.ANY)
    hbm = pl.BlockSpec(memory_space=pltpu.HBM)
    vmem = pl.BlockSpec(memory_space=pltpu.VMEM)
    smem = pl.BlockSpec(memory_space=pltpu.SMEM)
    a_shape = jax.ShapeDtypeStruct((hops_all, rb * bs, rb * bs), jnp.bfloat16)
    t_shape = jax.ShapeDtypeStruct((rb * bs, (span + 1) * bs), jnp.float32)
    o_shape = jax.ShapeDtypeStruct((rb, m_count, bs, bs), jnp.bfloat16)
    n_shape = jax.ShapeDtypeStruct((NOTE, bs), jnp.int32)

    edges = chunk_bounds(rb * slots)
    n = len(edges) - 1
    near, far_y, far_z, side_y, side_z = ([None] * n for _ in range(5))
    state = {}

    def add(index, own=False, last=False, **far):
        first = own
        noted = {}
        inputs, pieces = [], []
        if own:
            inputs.append(("cols_own", smem, b_cols))
            pieces.append(("own", 0, rb * slots, "own", None))
        else:
            inputs.append(("notes_like", smem, c_cols if last else b_cols))
        for kind, sources in (
            ("near", (near,)),
            ("far_y", (far_y,)),
            ("far_z", (far_z,)),
            ("side", (side_y, side_z)),
        ):
            if far.get(kind) and kind in state:
                inputs.append((f"note_{kind}", smem, state[kind]))
            for r in far.get(kind, ()):
                used = [f"{kind}{r}_{j}" for j in range(len(sources))]
                inputs += [(name, vmem, source[r]) for name, source in zip(used, sources)]
                if r == 0:
                    noted[kind] = tuple(used)
                used.append(None)
                pieces.append((kind, edges[r], edges[r + 1] - edges[r], used[0], used[1]))
        scratch = []
        if first:
            inputs.append(("a_cols", smem, a_cols.transpose(2, 0, 1)))
            inputs.append(("a_blocks", hbm, in_hbm(a_blocks)))
            inputs.append(("b_hbm", hbm, in_hbm(flat_b)))
            outputs = [("a_dense", vmem, a_shape), ("total", vmem, t_shape)]
            scratch = [
                ("own", pltpu.VMEM(flat_b.shape, flat_b.dtype)),
                ("a_sem", pltpu.SemaphoreType.DMA),
                ("b_sem", pltpu.SemaphoreType.DMA),
            ]
        else:
            inputs.append(("a_dense", vmem, state["a_dense"]))
            inputs.append(("total", vmem, state["total"]))
            outputs = [("total_out", vmem, t_shape)]
        for kind in noted:
            outputs.append((f"out_{kind}", vmem, n_shape))
            scratch.append((f"note_{kind}", pltpu.SMEM(n_shape.shape, n_shape.dtype)))
        if noted:
            scratch.append(("n_sem", pltpu.SemaphoreType.DMA))
        if last:
            inputs.append(("c_cols", smem, c_cols))
            outputs = [("out", hbm, o_shape)]
            scratch = [
                ("staged", pltpu.VMEM(o_shape.shape, o_shape.dtype)),
                ("o_sem", pltpu.SemaphoreType.DMA((rb,))),
            ]
        names = [x[0] for x in inputs + outputs + scratch]
        alias = {} if first or last else {names.index("total"): 0}
        blocks = sum(p[2] for p in pieces)
        results = pl.pallas_call(
            functools.partial(add_kernel, pieces, names, first, last, noted, d_count, rb),
            out_shape=[x[2] for x in outputs],
            in_specs=[x[1] for x in inputs],
            out_specs=[x[1] for x in outputs],
            scratch_shapes=[x[1] for x in scratch],
            input_output_aliases=alias,
            compiler_params=pltpu.CompilerParams(vmem_limit_bytes=24 * 1024 * 1024),
            cost_estimate=pl.CostEstimate(
                flops=COST * (blocks + 15), bytes_accessed=0, transcendentals=0
            ),
            name=f"add_{index}",
        )(*[x[2] for x in inputs])
        if first:
            state["a_dense"], state["total"] = results
        else:
            state["total"] = results[0]
            for kind, result in zip(noted, results[1:]):
                state[kind] = result

    def cut(source, r):
        return source[edges[r] : edges[r + 1]].reshape(-1, bs)

    def tie(x, *keys):
        places = [k if isinstance(k, tuple) else (state, k) for k in keys]
        tied = after((x, *[box[k] for box, k in places]))
        for (box, k), value in zip(places, tied[1:]):
            box[k] = value
        return tied[0]

    count = edges[1]
    packed = pl.pallas_call(
        functools.partial(pack_kernel, d_count, rb),
        out_shape=jax.ShapeDtypeStruct((count * bs + NOTE, bs), b_blocks.dtype),
        in_specs=[vmem, hbm],
        out_specs=vmem,
        scratch_shapes=[pltpu.SemaphoreType.DMA],
        cost_estimate=pl.CostEstimate(flops=COST, bytes_accessed=0, transcendentals=0),
        name="pack",
    )(b_cols, in_hbm(flat_b.reshape(-1, bs)))
    chunk = [packed, cut(flat_b, 1)] + [None] * (n - 2)

    def leave(r):
        near[r] = permuted(chunk[r], other_core)
        far_y[r] = permuted(chunk[r], across_y)

    leave(0)
    leave(1)
    add("own", own=True)
    for r in range(n):
        keys = [(far_y, r)]
        if r != 1:
            keys.append("total")
        if r >= 2:
            add(r - 2, near=(r - 2,), far_y=(r - 2,), far_z=(r - 2,), side=(r - 3,) if r >= 3 else ())
        move = far_y[r]
        if r + 2 < n:
            chunk[r + 2] = cut(tie(flat_b, *keys), r + 2)
            leave(r + 2)
            move = far_y[r]
        else:
            move = tie(move, "total")
        far_z[r] = permuted(move, across_z)
        side_y[r] = permuted(far_y[r], other_core)
        if r >= 1:
            side_z[r - 1] = permuted(far_z[r - 1], other_core)
    add(
        n - 2,
        near=(n - 2, n - 1),
        far_y=(n - 2, n - 1),
        far_z=(n - 2,),
        side=(n - 3,),
    )
    side_z[n - 1] = permuted(tie(far_z[n - 1], "total"), other_core)
    add(n - 1, last=True, far_z=(n - 1,), side=(n - 2, n - 1))
    return state["total"]


def solution(mesh):
    rows = P(("groups", "blk"))
    return jax.shard_map(
        per_device,
        mesh=mesh,
        in_specs=(rows,) * 5,
        out_specs=rows,
        check_vma=False,
    )
```

```python
import functools

import jax
import jax.numpy as jnp
from jax import lax
from jax.experimental import pallas as pl
from jax.experimental.pallas import tpu as pltpu
from jax.sharding import PartitionSpec as P

HOPS = 2
NOTE = 16
SHARES = (10, 14, 14, 14, 8)
COST_OWN, COST_NEAR, COST_MID, COST_END = 4600000000, 2300000000, 115000000, 345000000


AHEAD = 1


def plan(n):
    yield "Y", 0, ()
    yield "N", None, ()
    yield "Y", 1, ()
    yield "K", "own", ()
    for r in range(n):
        if r >= 2:
            yield "K", r - 2, ()
            yield "E", r - 2, ()
        if r + 2 < n:
            before = [("y", r)]
            if r == 0 or r == 2 or r >= 3:
                before.append(("k",))
            yield "Y", r + 2, tuple(before)
        before = []
        if r >= 2:
            before.append(("z", r - 2))
        yield "Z", r, tuple(before)
    yield "EY", n - 1, ()
    for r in range(n - 2, n - 1):
        if r == n - 2:
            yield "K", "near", ()
        yield "K", r, ()
        yield "E", r, ()
    yield "EZ", n - 1, (("k",),)
    yield "K", n - 1, ()


def permuted(block, route):
    count = lax.axis_size("blk")
    return lax.ppermute(block, "blk", [(i, route(i) % count) for i in range(count)])


def other_core(i):
    return i ^ 1


def across_y(i):
    return i ^ 2


def across_z(i):
    return i - 4 if i & 2 else i + 4


def chunk_bounds(total):
    edges = [0]
    for share in SHARES:
        edges.append(edges[-1] + share)
    return [e * total // edges[-1] for e in edges]


def pack_kernel(d_count, rb, cols_hbm, blocks, out, cols, out_sem, cols_sem):
    bs = blocks.shape[-1]
    slots = cols.shape[1]
    rows = out.shape[0] - NOTE
    copy = pltpu.make_async_copy(blocks.at[pl.ds(0, rows)], out.at[pl.ds(0, rows)], out_sem)
    fetch = pltpu.make_async_copy(cols_hbm, cols, cols_sem)
    copy.start()
    fetch.start()
    corner = (lax.axis_index("blk") - HOPS + d_count) % d_count * rb
    fetch.wait()
    at = cols[...] - corner
    at = jnp.where(at < 0, at + d_count * rb, at).astype(jnp.float32)
    at = jnp.concatenate([at, jnp.zeros((rb, bs - slots), jnp.float32)], axis=1)
    at = jnp.concatenate([at, jnp.zeros((NOTE - rb, bs), jnp.float32)], axis=0)
    out[rows : rows + NOTE, :] = at.astype(out.dtype)
    copy.wait()


def add_kernel(pieces, names, first, last, noted, mixed, d_count, rb, *refs):
    at = dict(zip(names, refs))
    a_dense, total = at["a_dense"], at["total"]
    bs = a_dense.shape[2] // rb
    span = (2 * HOPS + 1) * rb

    me = lax.axis_index("blk")
    core, y = me % 2, (me // 2) % 2
    corner = (me - HOPS + d_count) % d_count * rb

    def place(col):
        return (col - corner + d_count * rb) % (d_count * rb)

    def lanes(block):
        return pl.ds(pl.multiple_of(block * bs, bs), bs)

    hop_of = {
        "own": 0,
        "near": 1 - 2 * core,
        "far_y": 2 - 4 * y,
        "far_z": 4 * y - 2,
        "side": 2 * core - 1,
    }
    side_is_y = (y + core) % 2 == 1

    if first:
        a_blocks, a_cols, a_sem = at["a_blocks"], at["a_cols"], at["a_sem"]
        copies = [pltpu.make_async_copy(at["b_hbm"], at["local"], at["b_sem"])]
        copies[0].start()
        hops_all, sl = a_blocks.shape[1], a_blocks.shape[2]
        for h in range(hops_all):
            for i in range(rb):
                rows = pl.ds(i * bs, bs)
                gap = rb * (rb - 1) // 2
                for s in range(sl):
                    to = a_cols[s, i, h] % rb
                    gap -= to
                    copies.append(
                        pltpu.make_async_copy(
                            a_blocks.at[i, h, s], a_dense.at[h, rows, lanes(to)], a_sem
                        )
                    )
                    copies[-1].start()
                a_dense[h, rows, lanes(gap)] = jnp.zeros((bs, bs), a_dense.dtype)
        total[...] = jnp.zeros_like(total)
        for c in copies:
            c.wait()

    if "mix" in at:
        at["mix"][...] = jnp.where(side_is_y, at[mixed[1]][...], at[mixed[0]][...])

    fetches = []
    for kind in noted:
        notes = [
            at[name][at[name].shape[0] - NOTE :, :].astype(jnp.float32).astype(jnp.int32)
            for name in noted[kind]
        ]
        found = notes[0] if len(notes) == 1 else jnp.where(side_is_y, *notes)
        found = found + hop_of[kind] * rb
        found = jnp.where((found >= 0) & (found < span), found, span)
        at[f"out_{kind}"][...] = found
        fetches.append(pltpu.make_async_copy(at[f"out_{kind}"], at[f"note_{kind}"], at["n_sem"]))
        fetches[-1].start()
    for fetch in fetches:
        fetch.wait()

    for kind, begin, count, source, other in pieces:
        hop = hop_of[kind] + HOPS
        local = source == "local"
        slots = at["cols_local" if local else "notes_like"].shape[1]
        for n in range(count):
            row, slot = divmod(begin + n, slots)
            if local:
                to = jnp.minimum(place(at["cols_local"][row, slot]), span)
                block = at[source][n]
            else:
                to = at[f"note_{kind}"][row, slot]
                part = slice(n * bs, (n + 1) * bs)
                block = at[source][part, :]
                if other is not None:
                    block = jnp.where(side_is_y, block, at[other][part, :])
            total[:, lanes(to)] += jnp.dot(
                a_dense[hop, :, row * bs : (row + 1) * bs],
                block,
                preferred_element_type=jnp.float32,
            )

    if last:
        c_cols, staged = at["c_cols"], at["staged"]
        sends = []
        for i in range(rb):
            for m in range(c_cols.shape[1]):
                block = total[i * bs : (i + 1) * bs, lanes(place(c_cols[i, m]))]
                staged[i, m] = block.astype(staged.dtype)
            sends.append(pltpu.make_async_copy(staged.at[i], at["out"].at[i], at["o_sem"].at[i]))
            sends[-1].start()
        for c in sends:
            c.wait()


def per_device(a_blocks, a_cols, b_blocks, b_cols, c_cols):
    rb, hops_all, sl, bs, _ = a_blocks.shape
    m_count, slots = c_cols.shape[1], b_cols.shape[1]
    span = hops_all * rb
    d_count = lax.axis_size("blk")
    flat_b = b_blocks.reshape(rb * slots, bs, bs)
    after = lax.optimization_barrier
    in_hbm = functools.partial(pltpu.with_memory_space_constraint, memory_space=pltpu.HBM)

    any_space = pl.BlockSpec(memory_space=pl.ANY)
    hbm = pl.BlockSpec(memory_space=pltpu.HBM)
    vmem = pl.BlockSpec(memory_space=pltpu.VMEM)
    smem = pl.BlockSpec(memory_space=pltpu.SMEM)
    a_shape = jax.ShapeDtypeStruct((hops_all, rb * bs, rb * bs), jnp.bfloat16)
    t_shape = jax.ShapeDtypeStruct((rb * bs, (span + 1) * bs), jnp.float32)
    o_shape = jax.ShapeDtypeStruct((rb, m_count, bs, bs), jnp.bfloat16)
    n_shape = jax.ShapeDtypeStruct((NOTE, bs), jnp.int32)

    edges = chunk_bounds(rb * slots)
    n = len(edges) - 1
    near, far_y, far_z, side, side_y, side_z = ([None] * n for _ in range(6))
    chunk = [None] * n
    waiting = []
    state = {}

    def add(index, cost, local=None, last=False, mix=None, **far):
        first = local == "own"
        noted, mixed = {}, ()
        inputs, pieces = [], []
        if local:
            source, cols = (flat_b, b_cols) if first else (state["all_near"], state["near_cols"])
            inputs.append(("cols_local", smem, cols))
            inputs.append(("b_hbm", hbm, in_hbm(source)) if first else ("local", vmem, source))
            pieces.append((local, 0, rb * slots, "local", None))
        else:
            inputs.append(("notes_like", smem, c_cols if last else b_cols))
        for kind, sources in (
            ("near", (near,)),
            ("far_y", (far_y,)),
            ("far_z", (far_z,)),
            ("side", (side,)),
            ("last_side", (side_y, side_z)),
        ):
            name = "side" if kind == "last_side" else kind
            known = any(x[0] == f"note_{name}" for x in inputs)
            if far.get(kind) and name in state and not known:
                inputs.append((f"note_{name}", smem, state[name]))
            for r in far.get(kind, ()):
                used = [f"{kind}{r}_{j}" for j in range(len(sources))]
                inputs += [(label, vmem, source[r]) for label, source in zip(used, sources)]
                if r == 0:
                    noted[kind] = tuple(used)
                used.append(None)
                pieces.append((name, edges[r], edges[r + 1] - edges[r], used[0], used[1]))
        scratch = []
        if first:
            inputs.append(("a_cols", smem, a_cols.transpose(2, 0, 1)))
            inputs.append(("a_blocks", hbm, in_hbm(a_blocks)))
            outputs = [("a_dense", vmem, a_shape), ("total", vmem, t_shape)]
            scratch = [
                ("a_sem", pltpu.SemaphoreType.DMA),
            ]
        else:
            inputs.append(("a_dense", vmem, state["a_dense"]))
            inputs.append(("total", vmem, state["total"]))
            outputs = [("total_out", vmem, t_shape)]
        if first:
            scratch.append(("local", pltpu.VMEM(flat_b.shape, flat_b.dtype)))
            scratch.append(("b_sem", pltpu.SemaphoreType.DMA))
        for kind in noted:
            outputs.append((f"out_{kind}", vmem, n_shape))
            scratch.append((f"note_{kind}", pltpu.SMEM(n_shape.shape, n_shape.dtype)))
        if noted:
            scratch.append(("n_sem", pltpu.SemaphoreType.DMA))
        if mix is not None:
            have = [x[0] for x in inputs]
            if f"far_y{mix}_0" not in have:
                inputs.append((f"far_y{mix}_0", vmem, far_y[mix]))
            mixed = (f"far_y{mix}_0", f"far_z{mix}_0")
            outputs.append(("mix", vmem, jax.ShapeDtypeStruct(far_y[mix].shape, far_y[mix].dtype)))
        if last:
            inputs.append(("c_cols", smem, c_cols))
            outputs = [("out", hbm, o_shape)]
            scratch = [
                ("staged", pltpu.VMEM(o_shape.shape, o_shape.dtype)),
                ("o_sem", pltpu.SemaphoreType.DMA((rb,))),
            ]
        names = [x[0] for x in inputs + outputs + scratch]
        alias = {} if first or last else {names.index("total"): 0}
        results = pl.pallas_call(
            functools.partial(add_kernel, pieces, names, first, last, noted, mixed, d_count, rb),
            out_shape=[x[2] for x in outputs],
            in_specs=[x[1] for x in inputs],
            out_specs=[x[1] for x in outputs],
            scratch_shapes=[x[1] for x in scratch],
            input_output_aliases=alias,
            compiler_params=pltpu.CompilerParams(vmem_limit_bytes=24 * 1024 * 1024),
            cost_estimate=pl.CostEstimate(flops=cost, bytes_accessed=0, transcendentals=0),
            name=f"add_{index}",
        )(*[x[2] for x in inputs])
        if first:
            state["a_dense"], state["total"] = results
        else:
            state["total"] = results[0]
            for kind, result in zip(noted, results[1:]):
                state[kind] = result
            if mix is not None:
                state["mix", mix] = results[-1]

    def cut(source, r):
        return source[edges[r] : edges[r + 1]].reshape(-1, bs)

    def tie(x, *keys):
        if not keys:
            return x
        places = [k if isinstance(k, tuple) else (state, k) for k in keys]
        tied = after((x, *[box[k] for box, k in places]))
        for (box, k), value in zip(places, tied[1:]):
            box[k] = value
        return tied[0]

    count = edges[1]
    packed = pl.pallas_call(
        functools.partial(pack_kernel, d_count, rb),
        out_shape=jax.ShapeDtypeStruct((count * bs + NOTE, bs), b_blocks.dtype),
        in_specs=[hbm, hbm],
        out_specs=vmem,
        scratch_shapes=[
            pltpu.VMEM(b_cols.shape, b_cols.dtype),
            pltpu.SemaphoreType.DMA,
            pltpu.SemaphoreType.DMA,
        ],
        cost_estimate=pl.CostEstimate(flops=COST_MID, bytes_accessed=0, transcendentals=0),
        name="pack",
    )(in_hbm(b_cols), in_hbm(flat_b.reshape(-1, bs)))
    for kind, r, ties in plan(n):
        keys = ["total" if t[0] == "k" else ({"y": far_y, "z": far_z}[t[0]], t[1]) for t in ties]
        if kind == "N" and r is None:
            state["all_near"] = permuted(b_blocks, other_core).reshape(flat_b.shape)
            state["near_cols"] = permuted(b_cols, other_core)
        elif kind == "N":
            near[r] = permuted(chunk[r], other_core)
            waiting.append(r)
        elif kind == "Y":
            chunk[r] = packed if r == 0 else cut(tie(flat_b, *keys), r)
            far_y[r] = permuted(chunk[r], across_y)
        elif kind == "Z":
            far_z[r] = permuted(tie(far_y[r], *keys), across_z)
        elif kind == "E":
            side[r] = permuted(state["mix", r], other_core)
        elif kind == "EY":
            side_y[r] = permuted(tie(far_y[r], *keys), other_core)
        elif kind == "EZ":
            side_z[r] = permuted(tie(far_z[r], *keys), other_core)
        elif r in ("own", "near"):
            add(r, COST_OWN if r == "own" else COST_NEAR, local=r)
        elif r < n - 1:
            add(
                r,
                COST_MID if r < n - 2 else COST_END,
                mix=r,
                near=[w for w in waiting if w <= r + AHEAD or r == n - 2],
                far_y=(0, 1) if r == 0 else (r + 1,),
                far_z=(r,),
                side=(r - 1,) if r > 0 else (),
            )
            waiting = [w for w in waiting if w > r + AHEAD and r < n - 2]
        else:
            add(r, COST_MID, last=True, far_z=(r,), side=(r - 1,), last_side=(r,))
    return state["total"]


def solution(mesh):
    rows = P(("groups", "blk"))
    return jax.shard_map(
        per_device,
        mesh=mesh,
        in_specs=(rows,) * 5,
        out_specs=rows,
        check_vma=False,
    )
```

```python
import functools

import jax
import jax.numpy as jnp
from jax import lax
from jax.experimental import pallas as pl
from jax.experimental.pallas import tpu as pltpu
from jax.sharding import PartitionSpec as P

HOPS = 2
NOTE = 16
SHARES = (10, 14, 14, 14, 8)
COST_OWN, COST_NEAR, COST_MID, COST_END = 4600000000, 2300000000, 115000000, 345000000


AHEAD = 1


def plan(n):
    yield "Y", 0, ()
    yield "N", None, ()
    yield "Y", 1, ()
    yield "K", "own", ()
    for r in range(n):
        if r >= 2:
            yield "K", r - 2, ()
            yield "E", r - 2, ()
        if r + 2 < n:
            before = [("y", r)]
            if r == 0 or r == 2 or r >= 3:
                before.append(("k",))
            yield "Y", r + 2, tuple(before)
        before = []
        if r >= 2:
            before.append(("z", r - 2))
        yield "Z", r, tuple(before)
    yield "EY", n - 1, ()
    for r in range(n - 2, n - 1):
        if r == n - 2:
            yield "K", "near", ()
        yield "K", r, ()
        yield "E", r, ()
    yield "EZ", n - 1, (("k",),)
    yield "K", n - 1, ()


def permuted(block, route):
    count = lax.axis_size("blk")
    return lax.ppermute(block, "blk", [(i, route(i) % count) for i in range(count)])


def other_core(i):
    return i ^ 1


def across_y(i):
    return i ^ 2


def across_z(i):
    return i - 4 if i & 2 else i + 4


def chunk_bounds(total):
    edges = [0]
    for share in SHARES:
        edges.append(edges[-1] + share)
    return [e * total // edges[-1] for e in edges]


def pack_kernel(d_count, rb, cols_hbm, blocks, out, cols, out_sem, cols_sem):
    bs = blocks.shape[-1]
    slots = cols.shape[1]
    rows = out.shape[0] - NOTE
    copy = pltpu.make_async_copy(blocks.at[pl.ds(0, rows)], out.at[pl.ds(0, rows)], out_sem)
    fetch = pltpu.make_async_copy(cols_hbm, cols, cols_sem)
    copy.start()
    fetch.start()
    corner = (lax.axis_index("blk") - HOPS + d_count) % d_count * rb
    fetch.wait()
    at = cols[...] - corner
    at = jnp.where(at < 0, at + d_count * rb, at).astype(jnp.float32)
    at = jnp.concatenate([at, jnp.zeros((rb, bs - slots), jnp.float32)], axis=1)
    at = jnp.concatenate([at, jnp.zeros((NOTE - rb, bs), jnp.float32)], axis=0)
    out[rows : rows + NOTE, :] = at.astype(out.dtype)
    copy.wait()


def add_kernel(pieces, names, first, last, noted, mixed, d_count, rb, *refs):
    at = dict(zip(names, refs))
    a_dense, total = at["a_dense"], at["total"]
    bs = a_dense.shape[2] // rb
    span = (2 * HOPS + 1) * rb

    me = lax.axis_index("blk")
    core, y = me % 2, (me // 2) % 2
    corner = (me - HOPS + d_count) % d_count * rb

    def place(col):
        ahead = col - corner
        return jnp.where(ahead < 0, ahead + d_count * rb, ahead)

    def lanes(block):
        return pl.ds(pl.multiple_of(block * bs, bs), bs)

    hop_of = {
        "own": 0,
        "near": 1 - 2 * core,
        "far_y": 2 - 4 * y,
        "far_z": 4 * y - 2,
        "side": 2 * core - 1,
    }
    side_is_y = (y + core) % 2 == 1

    if first:
        a_blocks, a_cols, a_sem = at["a_blocks"], at["a_cols"], at["a_sem"]
        copies = [pltpu.make_async_copy(at["b_hbm"], at["local"], at["b_sem"])]
        copies[0].start()
        hops_all, sl = a_blocks.shape[1], a_blocks.shape[2]
        for h in range(hops_all):
            for i in range(rb):
                rows = pl.ds(i * bs, bs)
                gap = rb * (rb - 1) // 2
                for s in range(sl):
                    to = a_cols[s, i, h] % rb
                    gap -= to
                    copies.append(
                        pltpu.make_async_copy(
                            a_blocks.at[i, h, s], a_dense.at[h, rows, lanes(to)], a_sem
                        )
                    )
                    copies[-1].start()
                a_dense[h, rows, lanes(gap)] = jnp.zeros((bs, bs), a_dense.dtype)
        total[...] = jnp.zeros_like(total)
        for c in copies:
            c.wait()

    if "mix" in at:
        at["mix"][...] = jnp.where(side_is_y, at[mixed[1]][...], at[mixed[0]][...])

    fetches = []
    for kind in noted:
        notes = [
            at[name][at[name].shape[0] - NOTE :, :].astype(jnp.float32).astype(jnp.int32)
            for name in noted[kind]
        ]
        found = notes[0] if len(notes) == 1 else jnp.where(side_is_y, *notes)
        found = found + hop_of[kind] * rb
        found = jnp.where((found >= 0) & (found < span), found, span)
        at[f"out_{kind}"][...] = found
        fetches.append(pltpu.make_async_copy(at[f"out_{kind}"], at[f"note_{kind}"], at["n_sem"]))
        fetches[-1].start()
    for fetch in fetches:
        fetch.wait()

    for kind, begin, count, source, other in pieces:
        hop = hop_of[kind] + HOPS
        local = source == "local"
        slots = at["cols_local" if local else "notes_like"].shape[1]
        for n in range(count):
            row, slot = divmod(begin + n, slots)
            if local:
                to = jnp.minimum(place(at["cols_local"][row, slot]), span)
                block = at[source][n]
            else:
                to = at[f"note_{kind}"][row, slot]
                part = slice(n * bs, (n + 1) * bs)
                block = at[source][part, :]
                if other is not None:
                    block = jnp.where(side_is_y, block, at[other][part, :])
            total[:, lanes(to)] += jnp.dot(
                a_dense[hop, :, row * bs : (row + 1) * bs],
                block,
                preferred_element_type=jnp.float32,
            )

    if last:
        c_cols, staged = at["c_cols"], at["staged"]
        sends = []
        for i in range(rb):
            for m in range(c_cols.shape[1]):
                block = total[i * bs : (i + 1) * bs, lanes(place(c_cols[i, m]))]
                staged[i, m] = block.astype(staged.dtype)
            sends.append(pltpu.make_async_copy(staged.at[i], at["out"].at[i], at["o_sem"].at[i]))
            sends[-1].start()
        for c in sends:
            c.wait()


def per_device(a_blocks, a_cols, b_blocks, b_cols, c_cols):
    rb, hops_all, sl, bs, _ = a_blocks.shape
    m_count, slots = c_cols.shape[1], b_cols.shape[1]
    span = hops_all * rb
    d_count = lax.axis_size("blk")
    flat_b = b_blocks.reshape(rb * slots, bs, bs)
    after = lax.optimization_barrier
    in_hbm = functools.partial(pltpu.with_memory_space_constraint, memory_space=pltpu.HBM)

    any_space = pl.BlockSpec(memory_space=pl.ANY)
    hbm = pl.BlockSpec(memory_space=pltpu.HBM)
    vmem = pl.BlockSpec(memory_space=pltpu.VMEM)
    smem = pl.BlockSpec(memory_space=pltpu.SMEM)
    a_shape = jax.ShapeDtypeStruct((hops_all, rb * bs, rb * bs), jnp.bfloat16)
    t_shape = jax.ShapeDtypeStruct((rb * bs, (span + 1) * bs), jnp.float32)
    o_shape = jax.ShapeDtypeStruct((rb, m_count, bs, bs), jnp.bfloat16)
    n_shape = jax.ShapeDtypeStruct((NOTE, bs), jnp.int32)

    edges = chunk_bounds(rb * slots)
    n = len(edges) - 1
    near, far_y, far_z, side, side_y, side_z = ([None] * n for _ in range(6))
    chunk = [None] * n
    waiting = []
    state = {}

    def add(index, cost, local=None, last=False, mix=None, **far):
        first = local == "own"
        noted, mixed = {}, ()
        inputs, pieces = [], []
        if local:
            source, cols = (flat_b, b_cols) if first else (state["all_near"], state["near_cols"])
            inputs.append(("cols_local", smem, cols))
            inputs.append(("b_hbm", hbm, in_hbm(source)) if first else ("local", vmem, source))
            pieces.append((local, 0, rb * slots, "local", None))
        else:
            inputs.append(("notes_like", smem, c_cols if last else b_cols))
        for kind, sources in (
            ("near", (near,)),
            ("far_y", (far_y,)),
            ("far_z", (far_z,)),
            ("side", (side,)),
            ("last_side", (side_y, side_z)),
        ):
            name = "side" if kind == "last_side" else kind
            known = any(x[0] == f"note_{name}" for x in inputs)
            if far.get(kind) and name in state and not known:
                inputs.append((f"note_{name}", smem, state[name]))
            for r in far.get(kind, ()):
                used = [f"{kind}{r}_{j}" for j in range(len(sources))]
                inputs += [(label, vmem, source[r]) for label, source in zip(used, sources)]
                if r == 0:
                    noted[kind] = tuple(used)
                used.append(None)
                pieces.append((name, edges[r], edges[r + 1] - edges[r], used[0], used[1]))
        scratch = []
        if first:
            inputs.append(("a_cols", smem, a_cols.transpose(2, 0, 1)))
            inputs.append(("a_blocks", hbm, in_hbm(a_blocks)))
            outputs = [("a_dense", vmem, a_shape), ("total", vmem, t_shape)]
            scratch = [
                ("a_sem", pltpu.SemaphoreType.DMA),
            ]
        else:
            inputs.append(("a_dense", vmem, state["a_dense"]))
            inputs.append(("total", vmem, state["total"]))
            outputs = [("total_out", vmem, t_shape)]
        if first:
            scratch.append(("local", pltpu.VMEM(flat_b.shape, flat_b.dtype)))
            scratch.append(("b_sem", pltpu.SemaphoreType.DMA))
        for kind in noted:
            outputs.append((f"out_{kind}", vmem, n_shape))
            scratch.append((f"note_{kind}", pltpu.SMEM(n_shape.shape, n_shape.dtype)))
        if noted:
            scratch.append(("n_sem", pltpu.SemaphoreType.DMA))
        if mix is not None:
            have = [x[0] for x in inputs]
            if f"far_y{mix}_0" not in have:
                inputs.append((f"far_y{mix}_0", vmem, far_y[mix]))
            mixed = (f"far_y{mix}_0", f"far_z{mix}_0")
            outputs.append(("mix", vmem, jax.ShapeDtypeStruct(far_y[mix].shape, far_y[mix].dtype)))
        if last:
            inputs.append(("c_cols", smem, c_cols))
            outputs = [("out", hbm, o_shape)]
            scratch = [
                ("staged", pltpu.VMEM(o_shape.shape, o_shape.dtype)),
                ("o_sem", pltpu.SemaphoreType.DMA((rb,))),
            ]
        names = [x[0] for x in inputs + outputs + scratch]
        alias = {} if first or last else {names.index("total"): 0}
        results = pl.pallas_call(
            functools.partial(add_kernel, pieces, names, first, last, noted, mixed, d_count, rb),
            out_shape=[x[2] for x in outputs],
            in_specs=[x[1] for x in inputs],
            out_specs=[x[1] for x in outputs],
            scratch_shapes=[x[1] for x in scratch],
            input_output_aliases=alias,
            compiler_params=pltpu.CompilerParams(vmem_limit_bytes=24 * 1024 * 1024),
            cost_estimate=pl.CostEstimate(flops=cost, bytes_accessed=0, transcendentals=0),
            name=f"add_{index}",
        )(*[x[2] for x in inputs])
        if first:
            state["a_dense"], state["total"] = results
        else:
            state["total"] = results[0]
            for kind, result in zip(noted, results[1:]):
                state[kind] = result
            if mix is not None:
                state["mix", mix] = results[-1]

    def cut(source, r):
        return source[edges[r] : edges[r + 1]].reshape(-1, bs)

    def tie(x, *keys):
        if not keys:
            return x
        places = [k if isinstance(k, tuple) else (state, k) for k in keys]
        tied = after((x, *[box[k] for box, k in places]))
        for (box, k), value in zip(places, tied[1:]):
            box[k] = value
        return tied[0]

    count = edges[1]
    packed = pl.pallas_call(
        functools.partial(pack_kernel, d_count, rb),
        out_shape=jax.ShapeDtypeStruct((count * bs + NOTE, bs), b_blocks.dtype),
        in_specs=[hbm, hbm],
        out_specs=vmem,
        scratch_shapes=[
            pltpu.VMEM(b_cols.shape, b_cols.dtype),
            pltpu.SemaphoreType.DMA,
            pltpu.SemaphoreType.DMA,
        ],
        cost_estimate=pl.CostEstimate(flops=COST_MID, bytes_accessed=0, transcendentals=0),
        name="pack",
    )(in_hbm(b_cols), in_hbm(flat_b.reshape(-1, bs)))
    for kind, r, ties in plan(n):
        keys = ["total" if t[0] == "k" else ({"y": far_y, "z": far_z}[t[0]], t[1]) for t in ties]
        if kind == "N" and r is None:
            state["all_near"] = permuted(b_blocks, other_core).reshape(flat_b.shape)
            state["near_cols"] = permuted(b_cols, other_core)
        elif kind == "N":
            near[r] = permuted(chunk[r], other_core)
            waiting.append(r)
        elif kind == "Y":
            chunk[r] = packed if r == 0 else cut(tie(flat_b, *keys), r)
            far_y[r] = permuted(chunk[r], across_y)
        elif kind == "Z":
            far_z[r] = permuted(tie(far_y[r], *keys), across_z)
        elif kind == "E":
            side[r] = permuted(state["mix", r], other_core)
        elif kind == "EY":
            side_y[r] = permuted(tie(far_y[r], *keys), other_core)
        elif kind == "EZ":
            side_z[r] = permuted(tie(far_z[r], *keys), other_core)
        elif r in ("own", "near"):
            add(r, COST_OWN if r == "own" else COST_NEAR, local=r)
        elif r < n - 1:
            add(
                r,
                COST_MID if r < n - 2 else COST_END,
                mix=r,
                near=[w for w in waiting if w <= r + AHEAD or r == n - 2],
                far_y=(0, 1) if r == 0 else (r + 1,),
                far_z=(r,),
                side=(r - 1,) if r > 0 else (),
            )
            waiting = [w for w in waiting if w > r + AHEAD and r < n - 2]
        else:
            add(r, COST_MID, last=True, far_z=(r,), side=(r - 1,), last_side=(r,))
    return state["total"]


def solution(mesh):
    rows = P(("groups", "blk"))
    return jax.shard_map(
        per_device,
        mesh=mesh,
        in_specs=(rows,) * 5,
        out_specs=rows,
        check_vma=False,
    )
```
